256 devices in a mesh: cal: 64 (over z, y, core), gr: 4 (over x).
Axes of the slice: x: 4, y: 4, z: 8, core: 2. Of those that a mesh axis runs over, the one named last changes fastest.
Arguments:
- features: bfloat16 [131072, 4096], P('cal', 'gr'), may hold values from -6 to 6
- coef: bfloat16 [4096], P('gr'), may hold values from -0.09375 to 0.09375
- log_exposure: float32 [131072], P('cal'), may hold values from -0.7 to 0.7
- claims: float32 [131072], P('cal'), may hold values from 0 to 4
- cluster_id: int32 [131072], P('cal'), may hold values from 0 to 1023
- period: int32 [131072], P('cal'), may hold values from 0 to 127, as said below
- period_effect: float32 [128], replicated, may hold values from -0.5 to 0.5
Outputs:
- meat: float32 [4096, 4096], P('cal', 'gr')
The draws below stay inside these ranges and needn't reach their ends.
Inputs may be any that keep to these rules, and one draw needn't show every extreme that they name: `period`: rows of index d of cal lie in periods d * 2 to (d + 1) * 2 - 1.
All inputs are finite; a program needn't handle non-finite values.
Results may differ from the reference program's by a relative error of at most 0.0044.
Values sent between devices are 32-bit elements; how exact they have to be, the bound alone decides.
A program may use at most 64 MiB of HBM per device.

```python
import math
import jax
import jax.numpy as jnp
import numpy as np
from jax import lax

P_SIZE = 4096
ROWS_DEV = 2048
PER_DEV = 2
ROWS = 131072
CLUSTERS = 1024
PERIODS = 128


def draw_period(key, part):
    base = jnp.arange(ROWS, dtype=jnp.int32) // ROWS_DEV * PER_DEV
    extra = jax.random.randint(key, (ROWS,), 0, PER_DEV, dtype=jnp.int32)
    return (base + extra).astype(jnp.int32)


def touch_ends(entries, own_key, least, largest):
    longest = entries.shape.index(max(entries.shape))
    spots = []
    for shift in (0, 1):
        where = [jax.random.randint(jax.random.fold_in(own_key, axis), (), 0, length) for axis, length in enumerate(entries.shape)]
        where[longest] = (where[longest] + shift) % entries.shape[longest]
        spots.append(tuple(where))
    return entries.at[spots[0]].set(least).at[spots[1]].set(largest)


def levels(key, shape, pieces, least, high):
    def one(dim, blocks):
        steps = jax.random.uniform(jax.random.fold_in(jax.random.fold_in(key, 6), dim), (blocks,), jnp.float32, least / len(pieces), high / len(pieces))
        return jnp.repeat(jnp.exp(steps), shape[dim] // blocks).reshape((-1,) + (1,) * (len(shape) - dim - 1))

    loudness = one(*pieces[0])
    for cut in pieces[1:]:
        loudness = loudness * one(*cut)
    return loudness


def rank_bounds(amount, slope):
    loads = [(1 << 20) // math.isqrt(standing ** slope) + 1 for standing in range(1, amount + 1)]
    spread = 1 + sum(loads) // (1 << 30)
    return np.cumsum(np.array([max(1, weight // spread) for weight in loads]))


def skewed_ids(stream_key, extent, amount, skew):
    grid = rank_bounds(amount, skew)
    ticket = jax.random.randint(jax.random.fold_in(stream_key, 1), extent, 0, int(grid[amount - 1]))
    rank = jnp.searchsorted(jnp.asarray(grid, jnp.int32), ticket, side="right")
    return jax.random.permutation(jax.random.fold_in(stream_key, 2), amount)[rank].astype(jnp.int32)


def normal_values(own_key, shape, spread, limit, pieces=(), held_as=jnp.bfloat16):
    values = spread * jax.random.normal(own_key, shape, jnp.float32)
    if pieces:
        values = values * levels(own_key, shape, pieces, -0.22, 0.18)
    return jnp.clip(values, -limit, limit).astype(held_as)


def setup_inputs(seed: int = 0) -> dict:
    key_of = jax.random.split(jax.random.key(seed), 8)
    features = normal_values(key_of[0], (ROWS, P_SIZE), 1.0, 6.0, ((0, 64), (1, 4)))
    coef = normal_values(key_of[1], (P_SIZE,), P_SIZE ** -0.5, 0.09375, ((0, 4),))
    log_exposure = jnp.clip(jax.random.uniform(key_of[2], (ROWS,), jnp.float32, -0.7, 0.7) * levels(key_of[2], (ROWS,), ((0, 64),), -0.4, 0.0), -0.7, 0.7)
    claims = jnp.clip(4.0 * jax.random.uniform(key_of[3], (ROWS,), jnp.float32) ** levels(key_of[3], (ROWS,), ((0, 64),), -0.2, 0.2), 0.0, 4.0)
    cluster_id = touch_ends(skewed_ids(key_of[4], (ROWS,), CLUSTERS, 1), jax.random.fold_in(key_of[4], 3), 0, CLUSTERS - 1).astype(jnp.int32)
    period = draw_period(jax.random.fold_in(key_of[7], 71), 0)
    period_effect = jnp.clip(jax.random.uniform(key_of[6], (PERIODS,), jnp.float32, -0.5, 0.5), -0.5, 0.5)
    return dict(features=features, coef=coef, log_exposure=log_exposure, claims=claims, cluster_id=cluster_id, period=period, period_effect=period_effect)


def reference(features, coef, log_exposure, claims, cluster_id, period, period_effect):
    linear = jnp.dot(features, coef, preferred_element_type=jnp.float32)
    table = jnp.where(period[:, None] == jnp.arange(PERIODS, dtype=jnp.int32)[None, :], period_effect[None, :], jnp.float32(0.0))
    shift = jnp.sum(table, axis=1)
    resid = (claims - jnp.exp(linear + log_exposure + shift)).astype(jnp.bfloat16)
    block = ROWS_DEV
    count = ROWS // block
    feats = features.reshape(count, block, P_SIZE)
    res_b = resid.reshape(count, block)
    ids_b = cluster_id.reshape(count, block)

    def step(carry, item):
        feat_blk, res_blk, id_blk = item
        weighted = feat_blk.astype(jnp.float32) * res_blk.astype(jnp.float32)[:, None]
        return carry + jax.ops.segment_sum(weighted, id_blk, num_segments=CLUSTERS), None

    score, _ = lax.scan(step, jnp.zeros((CLUSTERS, P_SIZE), jnp.float32), (feats, res_b, ids_b))
    meat = jnp.dot(score.T, score, precision=lax.Precision.HIGHEST, preferred_element_type=jnp.float32)
    return meat / jnp.float32(ROWS)
```

```python
import jax
import jax.numpy as jnp
from jax import lax
from jax.experimental import pallas as pl
from jax.experimental.pallas import tpu as pltpu
from jax.sharding import PartitionSpec as P

NZ, NY, NX = 8, 4, 4
ROWS = 2048
WIDTH = 1024
HALF = 512
FCH = 4
TILES = 4
F32 = jnp.float32
BF16 = jnp.bfloat16


def remote(src, dst, send, recv, cal, gr):
    return pltpu.make_async_remote_copy(
        src_ref=src,
        dst_ref=dst,
        send_sem=send,
        recv_sem=recv,
        device_id=(cal, gr),
        device_id_type=pl.DeviceIdType.MESH,
    )


def split(v):
    hi = v.astype(BF16)
    lo = (v - hi.astype(F32)).astype(BF16)
    return hi, lo


def kernel(
    feat_hbm, coef_ref, logexp_ref, claims_ref, ids_ref, period_ref, effect_ref, out_ref,
    feat, cbuf, lin, res, picks, theirs, mine, core_rx, rx1, rx2, full, left, mpart, mrx,
    feat_sem, lin_send, lin_recv, core_send, core_recv,
    r1s, r1r, r2s, r2r, g1s, g1r, g2s, g2r, fws, fwr, m_send, m_recv,
):
    c = lax.axis_index("cal")
    x = lax.axis_index("gr")
    core = lax.rem(c, 2)
    y = lax.rem(lax.div(c, 2), NY)
    z = lax.div(c, 2 * NY)
    sib = c + 1 - 2 * core

    def cal_of(zz, yy):
        return (zz * NY + yy) * 2 + core

    fetches = []
    fr = ROWS // FCH
    for k in range(FCH):
        f = pltpu.make_async_copy(
            feat_hbm.at[pl.ds(k * fr, fr)], feat.at[pl.ds(k * fr, fr)], feat_sem.at[k]
        )
        f.start()
        fetches.append(f)

    barrier = pltpu.get_barrier_semaphore()
    peers = [(sib, x)]
    peers += [(c, lax.rem(x + k, NX)) for k in range(1, NX)]
    peers += [(cal_of(z, lax.rem(y + k, NY)), x) for k in (1, NY - 1)]
    peers += [(cal_of(lax.rem(z + k, NZ), y), x) for k in (1, NZ - 1)]
    for cal, gr in peers:
        pl.semaphore_signal(
            barrier, inc=1, device_id=(cal, gr), device_id_type=pl.DeviceIdType.MESH
        )

    cf = coef_ref[...].astype(F32)
    for j in range(WIDTH // 128):
        cbuf[:, j * 128 : (j + 1) * 128] = jnp.broadcast_to(cf[j : j + 1, :], (16, 128)).astype(BF16)
    for k in range(FCH):
        fetches[k].wait()
        part = lax.dot_general(
            cbuf[...], feat[k * fr : (k + 1) * fr, :], (((1,), (1,)), ((), ())),
            preferred_element_type=F32,
        )
        for j in range(fr // 128):
            lin[x, k * (fr // 128) + j, :] = part[0, j * 128 : (j + 1) * 128]
    pl.semaphore_wait(barrier, len(peers))

    sends = []
    for k in range(1, NX):
        s = remote(lin.at[x], lin.at[x], lin_send.at[k - 1], lin_recv.at[k - 1], c, lax.rem(x + k, NX))
        s.start()
        sends.append(s)
    eff = effect_ref[...]
    where = lax.broadcasted_iota(jnp.int32, (1, 128), 1)
    d = c * 2
    e0 = jnp.sum(jnp.where(where == d, eff, 0.0), axis=1, keepdims=True)
    e1 = jnp.sum(jnp.where(where == d + 1, eff, 0.0), axis=1, keepdims=True)
    per = period_ref[...]
    shift = jnp.where(per == d, e0, jnp.where(per == d + 1, e1, 0.0))
    for k in range(1, NX):
        src = lax.rem(x + NX - k, NX)
        remote(lin.at[src], lin.at[src], lin_send.at[k - 1], lin_recv.at[k - 1], c, x).wait_recv()
    linear = lin[0] + lin[1] + lin[2] + lin[3]
    value = claims_ref[...] - jnp.exp(linear + logexp_ref[...] + shift)
    res[...] = value.astype(BF16).astype(F32)

    def scores(base, dst, after):
        def build(j, carry):
            row = lax.broadcasted_iota(jnp.int32, (HALF, 128), 0) + base
            hit = row == ids_ref[pl.ds(j, 1), :]
            col = pl.ds(pl.multiple_of(j * 128, 128), 128)
            picks[:, col] = jnp.where(hit, res[pl.ds(j, 1), :], 0.0).astype(BF16)
            return carry

        lax.fori_loop(0, ROWS // 128, build, 0)
        w = WIDTH // TILES
        for n in range(TILES):
            dst[:, n * w : (n + 1) * w] = jnp.dot(
                picks[...], feat[:, n * w : (n + 1) * w], preferred_element_type=F32
            )
            after(n, pl.ds(n * w, w))

    def push(n, cols):
        s = remote(theirs.at[:, cols], core_rx.at[:, cols], core_send.at[n], core_recv.at[n], sib, x)
        s.start()
        sends.append(s)

    scores((1 - core) * HALF, theirs, push)

    def fold(n, cols):
        remote(theirs.at[:, cols], core_rx.at[:, cols], core_send.at[n], core_recv.at[n], sib, x).wait_recv()
        w = WIDTH // TILES
        mine[:, n * w : (n + 1) * w] += core_rx[:, n * w : (n + 1) * w]

    scores(core * HALF, mine, fold)
    for s in sends:
        s.wait_send()

    owner_x = lax.div(z, 2)
    lcol = pl.multiple_of((lax.rem(z, 2) * NY + y) * 128, 128)

    def plane(first, second):
        (n1, p1, dev1), (n2, p2, dev2) = first, second
        b1 = HALF // n1
        b2 = b1 // n2

        def reduce_ring(n, p, dev, base, rows, rx, ss, rs):
            h = n // 2
            started = []
            slot = [0] + [rows // 2 + i * rows for i in range(h - 1)]
            for s in range(h):
                dist = h - s
                for w in (0, 1):
                    step = n - dist if w == 0 else dist
                    target = base + lax.rem(p + step, n) * rows
                    size = rows
                    if s == 0:
                        size = rows // 2
                        target = target + w * size
                    target = pl.multiple_of(target, 8)
                    if s > 0:
                        prev = rows // 2 if s == 1 else rows
                        got = rx.at[w, pl.ds(slot[s - 1], prev)]
                        remote(got, got, ss.at[w, s - 1], rs.at[w, s - 1], c, x).wait_recv()
                        at = target + (w * prev if s == 1 else 0)
                        at = pl.ds(pl.multiple_of(at, 8), prev)
                        mine[at, :] += got[...]
                    to = dev(lax.rem(p + (n - 1 if w == 0 else 1), n))
                    cp = remote(
                        mine.at[pl.ds(target, size)], rx.at[w, pl.ds(slot[s], size)],
                        ss.at[w, s], rs.at[w, s], to, x,
                    )
                    cp.start()
                    started.append(cp)
            own = pl.ds(pl.multiple_of(base + p * rows, 8), rows)
            for w in (0, 1):
                got = rx.at[w, pl.ds(slot[h - 1], rows)]
                remote(got, got, ss.at[w, h - 1], rs.at[w, h - 1], c, x).wait_recv()
                mine[own, :] += got[...]
            return started

        def gather_ring(n, p, dev, base, rows, ss, rs, arrived):
            h = n // 2
            started = []
            for s in range(h + 1):
                for w in (0, 1):
                    if s > 0:
                        step = s if w == 0 else n - s
                        size = rows if s < h else rows // 2
                        start = base + lax.rem(p + step, n) * rows
                        if s == h:
                            start = start + w * size
                        got = full.at[pl.ds(pl.multiple_of(start, 8), size)]
                        remote(got, got, ss.at[w, s - 1], rs.at[w, s - 1], c, x).wait_recv()
                    if s < h:
                        step = s if w == 0 else lax.rem(n - s, n)
                        size = rows if s < h - 1 else rows // 2
                        start = base + lax.rem(p + step, n) * rows
                        if s == h - 1:
                            start = start + w * size
                        blk = full.at[pl.ds(pl.multiple_of(start, 8), size)]
                        to = dev(lax.rem(p + (n - 1 if w == 0 else 1), n))
                        cp = remote(blk, blk, ss.at[w, s], rs.at[w, s], to, x)
                        cp.start()
                        started.append(cp)
                if s > 0:
                    arrived(s)
            return started

        started = reduce_ring(n1, p1, dev1, 0, b1, rx1, r1s, r1r)
        base = p1 * b1
        started += reduce_ring(n2, p2, dev2, base, b2, rx2, r2s, r2r)
        own = pl.ds(pl.multiple_of(base + p2 * b2, 8), b2)
        full[own, :] = mine[own, :]
        started += gather_ring(n2, p2, dev2, base, b2, g2s, g2r, lambda s: None)

        def forward(event, block, go):
            at = pl.ds(pl.multiple_of(block * b1, 8), b1)
            src = full.at[at, pl.ds(lcol, 128)]
            for k in range(1, NX):
                to = lax.rem(x + k, NX)
                cp = remote(src, left.at[at], fws.at[event, k - 1], fwr.at[event], c, to)
                if go == "start":
                    cp.start()
                else:
                    cp.wait_send()

        def blocks_of(s):
            if s == 0:
                return [(0, p1)]
            if s == n1 // 2:
                return [(n1 - 1, lax.rem(p1 + s, n1))]
            return [(2 * s - 1, lax.rem(p1 + s, n1)), (2 * s, lax.rem(p1 + n1 - s, n1))]

        def forward_all(s, go):
            @pl.when(x == owner_x)
            def _():
                for event, block in blocks_of(s):
                    forward(event, block, go)

        forward_all(0, "start")
        started += gather_ring(
            n1, p1, dev1, 0, b1, g1s, g1r, lambda s: forward_all(s, "start")
        )
        for cp in started:
            cp.wait_send()
        for s in range(n1 // 2 + 1):
            forward_all(s, "wait")

        @pl.when(x == owner_x)
        def _():
            left[...] = full[:, pl.ds(lcol, 128)]

        @pl.when(x != owner_x)
        def _():
            for s in range(n1 // 2 + 1):
                for event, block in blocks_of(s):
                    at = pl.ds(pl.multiple_of(block * b1, 8), b1)
                    remote(left.at[at], left.at[at], fws.at[event, 0], fwr.at[event], c, x).wait_recv()

    along_y = (NY, y, lambda q: cal_of(z, q))
    along_z = (NZ, z, lambda q: cal_of(q, y))

    @pl.when(core == 0)
    def _():
        plane(along_y, along_z)

    @pl.when(core == 1)
    def _():
        plane(along_z, along_y)

    lt = left[...].T
    lhi, llo = split(lt)
    lhs = jnp.concatenate([lhi, llo], axis=0)
    w = WIDTH // TILES
    for n in range(TILES):
        ghi, glo = split(full[:, n * w : (n + 1) * w])
        both = jnp.dot(lhs, ghi, preferred_element_type=F32)
        low = jnp.dot(lhi, glo, preferred_element_type=F32)
        term = both[:128] + (both[128:] + low)
        mpart[:, n * w : (n + 1) * w] = term
    ours = pl.ds(pl.multiple_of(core * 64, 64), 64)
    other = pl.ds(pl.multiple_of((1 - core) * 64, 64), 64)
    m = remote(mpart.at[other], mrx, m_send, m_recv, sib, x)
    m.start()
    m.wait()
    out_ref[...] = (mpart[ours, :] + mrx[...]) * F32(1.0 / 131072)


def per_device(features, coef, log_exposure, claims, cluster_id, period, period_effect):
    vmem = pl.BlockSpec(memory_space=pltpu.VMEM)
    dma = pltpu.SemaphoreType.DMA
    scratch = [
        pltpu.VMEM((ROWS, WIDTH), BF16),
        pltpu.VMEM((16, WIDTH), BF16),
        pltpu.VMEM((NX, 16, 128), F32),
        pltpu.VMEM((16, 128), F32),
        pltpu.VMEM((HALF, ROWS), BF16),
        pltpu.VMEM((HALF, WIDTH), F32),
        pltpu.VMEM((HALF, WIDTH), F32),
        pltpu.VMEM((HALF, WIDTH), F32),
        pltpu.VMEM((2, 224, WIDTH), F32),
        pltpu.VMEM((2, 56, WIDTH), F32),
        pltpu.VMEM((HALF, WIDTH), F32),
        pltpu.VMEM((HALF, 128), F32),
        pltpu.VMEM((128, WIDTH), F32),
        pltpu.VMEM((64, WIDTH), F32),
        dma((FCH,)),
        dma((NX - 1,)),
        dma((NX - 1,)),
        dma((TILES,)),
        dma((TILES,)),
    ]
    scratch += [dma((2, 4)) for _ in range(8)]
    scratch += [dma((8, NX - 1)), dma((8,)), dma, dma]
    return pl.pallas_call(
        kernel,
        out_shape=jax.ShapeDtypeStruct((64, WIDTH), F32),
        in_specs=[pl.BlockSpec(memory_space=pl.ANY)] + [vmem] * 6,
        out_specs=vmem,
        scratch_shapes=scratch,
        compiler_params=pltpu.CompilerParams(
            collective_id=0, has_side_effects=True, vmem_limit_bytes=56 << 20
        ),
    )(
        features,
        coef.reshape(8, 128),
        log_exposure.reshape(16, 128),
        claims.reshape(16, 128),
        cluster_id.reshape(16, 128),
        period.reshape(16, 128),
        period_effect.reshape(1, 128),
    )


def solution(mesh):
    placed = (P("cal", "gr"), P("gr"), P("cal"), P("cal"), P("cal"), P("cal"), P())
    return jax.shard_map(
        per_device, mesh=mesh, in_specs=placed, out_specs=P("cal", "gr"), check_vma=False
    )
```

```python
import jax
import jax.numpy as jnp
from jax import lax
from jax.experimental import pallas as pl
from jax.experimental.pallas import tpu as pltpu
from jax.sharding import PartitionSpec as P

NZ, NY, NX = 8, 4, 4
ROWS = 2048
WIDTH = 1024
HALF = 512
FCH = 4
CHUNKS = 2
CW = WIDTH // CHUNKS
RING4 = [[(2, 1, 0), (-2, -1, 1)], [(1, 0, None), (-1, 0, None)]]
DIRECT4 = [[(2, 0, None), (1, 0, None), (-1, 0, None)]]
RING8 = [[(4, 3, 0), (-4, -3, 1)]] + [[(k, k - 1, None), (-k, 1 - k, None)] for k in (3, 2, 1)]
THREE8 = [
    [(4, 2, 0), (-4, -2, 1), (3, 2, None), (-3, -2, None)],
    [(2, 1, None), (-2, -1, None)],
    [(1, 0, None), (-1, 0, None)],
]
TWO8 = [
    [(4, 2, 0), (-4, -2, 1), (3, 2, None), (-3, -2, None), (1, 0, None), (-1, 0, None)],
    [(2, 0, None), (-2, 0, None)],
]
DIRECT8 = [[(4, 0, None)] + [(s * k, 0, None) for k in (3, 2, 1) for s in (1, -1)]]
BIG = {"y": RING4, "z": RING8}
SMALL = {"y": DIRECT4, "z": TWO8}
FIRST = ("yyyy", "zzzz")
EDGES = 8
F32 = jnp.float32
SKEW = 0
BF16 = jnp.bfloat16


def remote(src, dst, send, recv, cal, gr):
    return pltpu.make_async_remote_copy(
        src_ref=src,
        dst_ref=dst,
        send_sem=send,
        recv_sem=recv,
        device_id=(cal, gr),
        device_id_type=pl.DeviceIdType.MESH,
    )


def split(v):
    hi = v.astype(BF16)
    lo = (v - hi.astype(F32)).astype(BF16)
    return hi, lo


def kernel(
    feat_hbm, coef_ref, logexp_ref, claims_ref, ids_ref, period_ref, effect_ref, out_ref,
    feat, cbuf, lin, res, picks, theirs, mine, core_rx, rx1, rx2, full, left, mpart, mrx,
    feat_sem, lin_send, lin_recv, core_send, core_recv,
    r1s, r1r, r2s, r2r, g1s, g1r, g2s, g2r, fws, fwr, m_send, m_recv,
):
    c = lax.axis_index("cal")
    x = lax.axis_index("gr")
    core = lax.rem(c, 2)
    y = lax.rem(lax.div(c, 2), NY)
    z = lax.div(c, 2 * NY)
    sib = c + 1 - 2 * core

    def cal_of(zz, yy):
        return (zz * NY + yy) * 2 + core

    fetches = []
    fr = ROWS // FCH
    for k in range(FCH):
        f = pltpu.make_async_copy(
            feat_hbm.at[pl.ds(k * fr, fr)], feat.at[pl.ds(k * fr, fr)], feat_sem.at[k]
        )
        f.start()
        fetches.append(f)

    barrier = pltpu.get_barrier_semaphore()
    peers = [(sib, x)]
    peers += [(c, lax.rem(x + k, NX)) for k in range(1, NX)]
    peers += [(cal_of(z, lax.rem(y + k, NY)), x) for k in range(1, NY)]
    peers += [(cal_of(lax.rem(z + k, NZ), y), x) for k in range(1, NZ)]
    for cal, gr in peers:
        pl.semaphore_signal(
            barrier, inc=1, device_id=(cal, gr), device_id_type=pl.DeviceIdType.MESH
        )

    cf = coef_ref[...].astype(F32)
    for j in range(WIDTH // 128):
        cbuf[:, j * 128 : (j + 1) * 128] = jnp.broadcast_to(cf[j : j + 1, :], (16, 128)).astype(BF16)
    for k in range(FCH):
        fetches[k].wait()
        part = lax.dot_general(
            cbuf[...], feat[k * fr : (k + 1) * fr, :], (((1,), (1,)), ((), ())),
            preferred_element_type=F32,
        )
        for j in range(fr // 128):
            lin[x, k * (fr // 128) + j, :] = part[0, j * 128 : (j + 1) * 128]
    pl.semaphore_wait(barrier, len(peers))

    for k in range(1, NX):
        to = lax.rem(x + k, NX)
        remote(lin.at[x], lin.at[x], lin_send.at[k - 1], lin_recv.at[k - 1], c, to).start()
    eff = effect_ref[...]
    where = lax.broadcasted_iota(jnp.int32, (1, 128), 1)
    d = c * 2
    e0 = jnp.sum(jnp.where(where == d, eff, 0.0), axis=1, keepdims=True)
    e1 = jnp.sum(jnp.where(where == d + 1, eff, 0.0), axis=1, keepdims=True)
    per = period_ref[...]
    shift = jnp.where(per == d, e0, jnp.where(per == d + 1, e1, 0.0))
    for k in range(1, NX):
        src = lax.rem(x + NX - k, NX)
        remote(lin.at[src], lin.at[src], lin_send.at[k - 1], lin_recv.at[k - 1], c, x).wait()
    linear = lin[0] + lin[1] + lin[2] + lin[3]
    value = claims_ref[...] - jnp.exp(linear + logexp_ref[...] + shift)
    res[...] = value.astype(BF16).astype(F32)

    def build(half, base):
        def column(j, carry):
            row = lax.broadcasted_iota(jnp.int32, (HALF, 128), 0) + base
            hit = row == ids_ref[pl.ds(j, 1), :]
            col = pl.ds(pl.multiple_of(j * 128, 128), 128)
            picks[half, :, col] = jnp.where(hit, res[pl.ds(j, 1), :], 0.0).astype(BF16)
            return carry

        lax.fori_loop(0, ROWS // 128, column, 0)

    def product(n, half, dst):
        dst[n] = jnp.dot(picks[half], feat[:, n * CW : (n + 1) * CW], preferred_element_type=F32)

    def push(n):
        return remote(theirs.at[n], core_rx.at[n], core_send.at[n], core_recv.at[n], sib, x)

    def fold(n):
        push(n).wait_recv()
        mine[n] += core_rx[n]

    owner_x = lax.div(z, 2)
    place = lax.rem(z, 2) * NY + y
    lchunk = lax.div(place, CW // 128)
    lcol = pl.multiple_of(lax.rem(place, CW // 128) * 128, 128)
    axes = {
        "y": (NY, y, lambda q: cal_of(z, q)),
        "z": (NZ, z, lambda q: cal_of(q, y)),
    }

    def rows_of(base, n, place, rows, half):
        start = base + lax.rem(place + 2 * n, n) * rows
        if half is not None:
            rows = rows // 2
            start = start + half * rows
        return pl.ds(pl.multiple_of(start, 8), rows)

    def slots_of(tree, rows):
        at, slots = 0, []
        for rnd in tree:
            for a, b, half in rnd:
                size = rows if half is None else rows // 2
                slots.append((a, b, half, pl.ds(at, size)))
                at += size
        return slots

    def plan(k, first):
        second = "z" if first == "y" else "y"
        n1, p1, dev1 = axes[first]
        n2, p2, dev2 = axes[second]
        b1 = HALF // n1
        b2 = b1 // n2
        base2 = p1 * b1
        steps, ends = [], []

        def sum_steps(tree, n, p, dev, base, rows, rx, ss, rs):
            slots = slots_of(tree, rows)

            def edge(i):
                a, b, half, slot = slots[i]
                blk = rows_of(base, n, p - a, rows, half)
                to = dev(lax.rem(p - a + b + 2 * n, n))
                return remote(mine.at[k, blk], rx.at[k, slot], ss.at[k, i], rs.at[k, i], to, x)

            def take(place):
                for i, (_, b, half, slot) in enumerate(slots):
                    if b == place:
                        edge(i).wait_recv()
                        mine[k, rows_of(base, n, p - b, rows, half), :] += rx[k, slot, :]

            def send(lo, hi):
                done = set()
                for i in range(lo, hi):
                    a = slots[i][0]
                    if a not in done:
                        done.add(a)
                        take(a)
                    edge(i).start()

            at = 0
            for rnd in tree:
                steps.append(lambda lo=at, hi=at + len(rnd): send(lo, hi))
                at += len(rnd)
            ends.extend(lambda i=i: edge(i).wait_send() for i in range(at))
            return lambda: take(0)

        def gather_steps(tree, n, p, dev, base, rows, ss, rs, got):
            slots = slots_of(tree, rows)

            def edge(i, receive=False):
                a, b, half, _ = slots[i]
                at = a if receive else b
                blk = rows_of(base, n, p - at, rows, half)
                to = dev(lax.rem(p - b + a + 2 * n, n))
                return remote(full.at[k, blk], full.at[k, blk], ss.at[k, i], rs.at[k, i], to, x)

            def take(place):
                for i, (a, _, _, _) in enumerate(slots):
                    if a == place:
                        edge(i, True).wait_recv()
                        got(place)

            def send(lo, hi):
                done = set()
                for i in range(lo, hi):
                    b = slots[i][1]
                    if b not in done:
                        done.add(b)
                        if b != 0:
                            take(b)
                    edge(i).start()

            at = len(slots)
            for rnd in reversed(tree):
                steps.append(lambda lo=at - len(rnd), hi=at: send(lo, hi))
                at -= len(rnd)
            ends.extend(lambda i=i: edge(i).wait_send() for i in range(len(slots)))

            def rest():
                inner = {b for _, b, _, _ in slots}
                seen = set()
                for a, _, _, _ in slots:
                    if a not in inner and a not in seen:
                        seen.add(a)
                        take(a)

            return rest

        def chain(done, more):
            def both():
                done()
                more()

            return both

        end1 = sum_steps(BIG[first], n1, p1, dev1, 0, b1, rx1, r1s, r1r)
        mark = len(steps)
        end2 = sum_steps(SMALL[second], n2, p2, dev2, base2, b2, rx2, r2s, r2r)
        steps[mark] = chain(end1, steps[mark])
        mark = len(steps)

        def own():
            end2()
            at = rows_of(base2, n2, p2, b2, None)
            full[k, at, :] = mine[k, at, :]

        end3 = gather_steps(SMALL[second], n2, p2, dev2, base2, b2, g2s, g2r, lambda place: None)
        steps[mark] = chain(own, steps[mark])
        mark = len(steps)

        sends = {}

        def forward(event, place, half):
            at = rows_of(0, n1, p1 - place, b1, half)
            src = full.at[k, at, pl.ds(lcol, 128)]
            return [
                remote(src, left.at[at], fws.at[event, q - 1], fwr.at[event], c, lax.rem(x + q, NX))
                for q in range(1, NX)
            ]

        mine_to_send = jnp.logical_and(x == owner_x, lchunk == k)
        mine_to_get = jnp.logical_and(x != owner_x, lchunk == k)

        def out(place):
            sends[place] = len(sends)

            @pl.when(mine_to_send)
            def _():
                for cp in forward(sends[place], place, None):
                    cp.start()

        slots1 = slots_of(BIG[first], b1)
        counts = {}
        for a, _, _, _ in slots1:
            key = a % n1
            counts[key] = counts.get(key, 0) + 1
        left_over = dict(counts)

        def got(place):
            key = place % n1
            left_over[key] -= 1
            if left_over[key] == 0:
                out(key)

        def begin():
            end3()
            out(0)

        end4 = gather_steps(BIG[first], n1, p1, dev1, 0, b1, g1s, g1r, got)
        steps[mark] = chain(begin, steps[mark])
        steps.append(end4)

        def finish():
            for e in ends:
                e()

            @pl.when(mine_to_send)
            def _():
                for place, event in sends.items():
                    for cp in forward(event, place, None):
                        cp.wait_send()
                left[...] = full[k, :, pl.ds(lcol, 128)]

            @pl.when(mine_to_get)
            def _():
                for place, event in sends.items():
                    at = rows_of(0, n1, p1 - place, b1, None)
                    remote(left.at[at], left.at[at], fws.at[event, 0], fwr.at[event], c, x).wait_recv()

        return steps, finish

    plans = [[plan(k, FIRST[h][k]) for k in range(CHUNKS)] for h in (0, 1)]

    def comm(k, s):
        for h in (0, 1):
            steps = plans[h][k][0]
            if s < len(steps):
                pl.when(core == h)(steps[s])

    build(0, (1 - core) * HALF)
    for k in range(CHUNKS):
        product(k, 0, theirs)
        push(k).start()
        if k == 0:
            build(1, core * HALF)
        product(k, 1, mine)
        if k > 0:
            fold(k - 1)
            comm(k - 1, 0)
        if k > 2:
            comm(k - 3, 1)
    fold(CHUNKS - 1)
    comm(CHUNKS - 1, 0)
    total = max(len(p[0]) for h in (0, 1) for p in plans[h])
    for s in range(1, total + SKEW * CHUNKS):
        for k in range(CHUNKS):
            at = s - SKEW * k
            if at >= (2 if k + 3 < CHUNKS else 1) and at < total:
                comm(k, at)
    for k in range(CHUNKS):
        push(k).wait_send()
        for h in (0, 1):
            pl.when(core == h)(plans[h][k][1])

    lt = left[...].T
    lhi, llo = split(lt)
    lhs = jnp.concatenate([lhi, llo], axis=0)
    for n in range(CHUNKS):
        ghi, glo = split(full[n])
        both = jnp.dot(lhs, ghi, preferred_element_type=F32)
        low = jnp.dot(lhi, glo, preferred_element_type=F32)
        mpart[:, n * CW : (n + 1) * CW] = both[:128] + (both[128:] + low)
    ours = pl.ds(pl.multiple_of(core * 64, 64), 64)
    other = pl.ds(pl.multiple_of((1 - core) * 64, 64), 64)
    m = remote(mpart.at[other], mrx, m_send, m_recv, sib, x)
    m.start()
    m.wait()
    out_ref[...] = (mpart[ours, :] + mrx[...]) * F32(1.0 / 131072)


def per_device(features, coef, log_exposure, claims, cluster_id, period, period_effect):
    vmem = pl.BlockSpec(memory_space=pltpu.VMEM)
    dma = pltpu.SemaphoreType.DMA
    chunked = pltpu.VMEM((CHUNKS, HALF, CW), F32)
    scratch = [
        pltpu.VMEM((ROWS, WIDTH), BF16),
        pltpu.VMEM((16, WIDTH), BF16),
        pltpu.VMEM((NX, 16, 128), F32),
        pltpu.VMEM((16, 128), F32),
        pltpu.VMEM((2, HALF, ROWS), BF16),
        chunked,
        chunked,
        chunked,
        pltpu.VMEM((CHUNKS, 448, CW), F32),
        pltpu.VMEM((CHUNKS, 112, CW), F32),
        chunked,
        pltpu.VMEM((HALF, 128), F32),
        pltpu.VMEM((128, WIDTH), F32),
        pltpu.VMEM((64, WIDTH), F32),
        dma((FCH,)),
        dma((NX - 1,)),
        dma((NX - 1,)),
        dma((CHUNKS,)),
        dma((CHUNKS,)),
    ]
    scratch += [dma((CHUNKS, EDGES)) for _ in range(8)]
    scratch += [dma((8, NX - 1)), dma((8,)), dma, dma]
    return pl.pallas_call(
        kernel,
        out_shape=jax.ShapeDtypeStruct((64, WIDTH), F32),
        in_specs=[pl.BlockSpec(memory_space=pl.ANY)] + [vmem] * 6,
        out_specs=vmem,
        scratch_shapes=scratch,
        compiler_params=pltpu.CompilerParams(
            collective_id=0, has_side_effects=True, vmem_limit_bytes=56 << 20
        ),
    )(
        features,
        coef.reshape(8, 128),
        log_exposure.reshape(16, 128),
        claims.reshape(16, 128),
        cluster_id.reshape(16, 128),
        period.reshape(16, 128),
        period_effect.reshape(1, 128),
    )


def solution(mesh):
    placed = (P("cal", "gr"), P("gr"), P("cal"), P("cal"), P("cal"), P("cal"), P())
    return jax.shard_map(
        per_device, mesh=mesh, in_specs=placed, out_specs=P("cal", "gr"), check_vma=False
    )
```

```python
import jax
import jax.numpy as jnp
from jax import lax
from jax.experimental import pallas as pl
from jax.experimental.pallas import tpu as pltpu
from jax.sharding import PartitionSpec as P

NZ, NY, NX = 8, 4, 4
ROWS = 2048
WIDTH = 1024
HALF = 512
FCH = 4
CHUNKS = 4
CW = WIDTH // CHUNKS
RING4 = [[(2, 1, 0), (-2, -1, 1)], [(1, 0, None), (-1, 0, None)]]
DIRECT4 = [[(2, 0, None), (1, 0, None), (-1, 0, None)]]
RING8 = [[(4, 3, 0), (-4, -3, 1)]] + [[(k, k - 1, None), (-k, 1 - k, None)] for k in (3, 2, 1)]
THREE8 = [
    [(4, 2, 0), (-4, -2, 1), (3, 2, None), (-3, -2, None)],
    [(2, 1, None), (-2, -1, None)],
    [(1, 0, None), (-1, 0, None)],
]
TWO8 = [
    [(4, 2, 0), (-4, -2, 1), (3, 2, None), (-3, -2, None), (1, 0, None), (-1, 0, None)],
    [(2, 0, None), (-2, 0, None)],
]
DIRECT8 = [[(4, 0, None)] + [(s * k, 0, None) for k in (3, 2, 1) for s in (1, -1)]]
BIG = {"y": RING4, "z": RING8}
SMALL = {"y": DIRECT4, "z": TWO8}
FIRST = "yz"
UNIT = 128
EDGES = 8
F32 = jnp.float32
UNROLL = 4
AHEAD = 1
ZPEERS = (1, 2, NZ - 2, NZ - 1)
BF16 = jnp.bfloat16


def order(n):
    return [n // 2] + [w * d % n for d in range(n // 2 - 1, 0, -1) for w in (1, -1)] + [0]


def remote(src, dst, send, recv, cal, gr):
    return pltpu.make_async_remote_copy(
        src_ref=src,
        dst_ref=dst,
        send_sem=send,
        recv_sem=recv,
        device_id=(cal, gr),
        device_id_type=pl.DeviceIdType.MESH,
    )


def split(v):
    hi = v.astype(BF16)
    lo = (v - hi.astype(F32)).astype(BF16)
    return hi, lo


def kernel(
    feat_hbm, coef_ref, logexp_ref, claims_ref, ids_ref, period_ref, effect_ref, out_ref,
    feat, cbuf, lin, res, picks, theirs, mine, core_rx, rx1, rx2, full, left, mpart, mrx,
    feat_sem, lin_send, lin_recv, core_send, core_recv,
    sum_send, gat_send, r1r, r2r, g1r, g2r, fws, fwr, m_send, m_recv,
):
    c = lax.axis_index("cal")
    x = lax.axis_index("gr")
    core = lax.rem(c, 2)
    y = lax.rem(lax.div(c, 2), NY)
    z = lax.div(c, 2 * NY)
    sib = c + 1 - 2 * core

    def cal_of(zz, yy):
        return (zz * NY + yy) * 2 + core

    fetches = []
    fr = ROWS // FCH
    for k in range(FCH):
        f = pltpu.make_async_copy(
            feat_hbm.at[pl.ds(k * fr, fr)], feat.at[pl.ds(k * fr, fr)], feat_sem.at[k]
        )
        f.start()
        fetches.append(f)

    barrier = pltpu.get_barrier_semaphore()
    peers = [(sib, x)]
    peers += [(c, lax.rem(x + k, NX)) for k in range(1, NX)]
    peers += [(cal_of(z, lax.rem(y + k, NY)), x) for k in range(1, NY)]
    peers += [(cal_of(lax.rem(z + k, NZ), y), x) for k in ZPEERS]
    for cal, gr in peers:
        pl.semaphore_signal(
            barrier, inc=1, device_id=(cal, gr), device_id_type=pl.DeviceIdType.MESH
        )

    cf = coef_ref[...].astype(F32)
    for j in range(WIDTH // 128):
        cbuf[:, j * 128 : (j + 1) * 128] = jnp.broadcast_to(cf[j : j + 1, :], (16, 128)).astype(BF16)
    for k in range(FCH):
        fetches[k].wait()
        part = lax.dot_general(
            cbuf[...], feat[k * fr : (k + 1) * fr, :], (((1,), (1,)), ((), ())),
            preferred_element_type=F32,
        )
        for j in range(fr // 128):
            lin[x, k * (fr // 128) + j, :] = part[0, j * 128 : (j + 1) * 128]
    pl.semaphore_wait(barrier, len(peers))

    for k in range(1, NX):
        to = lax.rem(x + k, NX)
        remote(lin.at[x], lin.at[x], lin_send.at[k - 1], lin_recv.at[k - 1], c, to).start()
    eff = effect_ref[...]
    where = lax.broadcasted_iota(jnp.int32, (1, 128), 1)
    d = c * 2
    e0 = jnp.sum(jnp.where(where == d, eff, 0.0), axis=1, keepdims=True)
    e1 = jnp.sum(jnp.where(where == d + 1, eff, 0.0), axis=1, keepdims=True)
    per = period_ref[...]
    shift = jnp.where(per == d, e0, jnp.where(per == d + 1, e1, 0.0))
    for k in range(1, NX):
        src = lax.rem(x + NX - k, NX)
        remote(lin.at[src], lin.at[src], lin_send.at[k - 1], lin_recv.at[k - 1], c, x).wait()
    linear = lin[0] + lin[1] + lin[2] + lin[3]
    value = claims_ref[...] - jnp.exp(linear + logexp_ref[...] + shift)
    res[...] = value.astype(BF16).astype(F32)

    ring_y = [lax.rem(y + k, NY) for k in range(NY)]
    ring_z = [lax.rem(z + k, NZ) for k in range(NZ)]
    axes = {
        "y": (NY, ring_y, [cal_of(z, q) for q in ring_y]),
        "z": (NZ, ring_z, [cal_of(q, y) for q in ring_z]),
    }

    def firsts(h):
        (n1, p1, _), (n2, p2, _) = axes[FIRST[h]], axes["z" if FIRST[h] == "y" else "y"]
        b1 = HALF // n1
        b2 = b1 // n2
        return [h * HALF + p1[d1] * b1 + p2[d2] * b2 for d1 in order(n1) for d2 in order(n2)]

    groups = [
        [jnp.where(core == half, v1, v0) for v0, v1 in zip(firsts(0), firsts(1))] for half in (0, 1)
    ]
    few = HALF // len(groups[0])

    def build(half, unit):
        def column(j, carry):
            row = lax.broadcasted_iota(jnp.int32, (few, 128), 0)
            ids = ids_ref[pl.ds(j, 1), :]
            val = jnp.broadcast_to(res[pl.ds(j, 1), :], (few, 128))
            col = pl.ds(pl.multiple_of(j * 128, 128), 128)
            for g in range(unit * UNIT // few, (unit + 1) * UNIT // few):
                hit = row == ids - groups[half][g]
                picks[half, g * few : (g + 1) * few, col] = jnp.where(hit, val, 0.0).astype(BF16)
            return carry

        lax.fori_loop(0, ROWS // 128, column, 0)

    def product(half, unit, dst):
        build(half, unit)
        here = slice(unit * UNIT, (unit + 1) * UNIT)
        for n in range(CHUNKS):
            dst[n, here, :] = jnp.dot(
                picks[half, here, :], feat[:, n * CW : (n + 1) * CW], preferred_element_type=F32
            )

    def push(u):
        here = pl.ds(u * UNIT, UNIT)
        return remote(
            theirs.at[:, here], core_rx.at[:, here], core_send.at[u], core_recv.at[u], sib, x
        )

    def make(u):
        product(0, u, theirs)
        push(u).start()
        product(1, u, mine)

    def fold(u):
        push(u).wait_recv()
        here = slice(u * UNIT, (u + 1) * UNIT)
        for n in range(CHUNKS):
            mine[n, here, :] += core_rx[n, here, :]

    owner_x = lax.div(z, 2)
    place = lax.rem(z, 2) * NY + y
    lchunk = lax.div(place, CW // 128)
    lcol = pl.multiple_of(lax.rem(place, CW // 128) * 128, 128)
    def rows_of(base, n, place, rows, half):
        start = base + order(n).index(place % n) * rows
        if half is not None:
            rows = rows // 2
            start = start + half * rows
        return pl.ds(start, rows)

    def slots_of(tree, rows):
        at, slots = 0, []
        for rnd in tree:
            for a, b, half in rnd:
                size = rows if half is None else rows // 2
                slots.append((a, b, half, pl.ds(at, size)))
                at += size
        return slots

    def add(k, start, rx, slot):
        def tile(j, carry):
            here = pl.ds(pl.multiple_of(start + j * 8, 8), 8)
            mine[k, here, :] += rx[k, pl.ds(pl.multiple_of(slot.start + j * 8, 8), 8), :]
            return carry

        lax.fori_loop(0, slot.size // 8, tile, 0, unroll=min(UNROLL, slot.size // 8))

    def plan(k, first):
        second = "z" if first == "y" else "y"
        n1, p1, dev1 = axes[first]
        n2, p2, dev2 = axes[second]
        b1 = HALF // n1
        b2 = b1 // n2
        base2 = HALF - b1
        needs = []
        steps = []

        def sum_steps(tree, n, p, dev, base, rows, rx, ss, rs):
            slots = slots_of(tree, rows)

            def edge(i):
                a, b, half, slot = slots[i]
                blk = rows_of(base, n, -a, rows, half)
                return remote(mine.at[k, blk], rx.at[k, slot], ss.at[k], rs.at[k, i], dev[(b - a) % n], x)

            def take(place):
                for i, (_, b, half, slot) in enumerate(slots):
                    if b == place:
                        edge(i).wait_recv()
                        add(k, rows_of(base, n, -b, rows, half).start, rx, slot)

            def send(lo, hi):
                done = set()
                for i in range(lo, hi):
                    a = slots[i][0]
                    if a not in done:
                        done.add(a)
                        take(a)
                    edge(i).start()

            at = 0
            for rnd in tree:
                blks = [rows_of(base, n, -a, rows, None) for a, _, _ in rnd]
                needs.append(max(blk.start + blk.size for blk in blks))
                steps.append(lambda lo=at, hi=at + len(rnd): send(lo, hi))
                at += len(rnd)
            return lambda: take(0)

        def gather_steps(tree, n, p, dev, base, rows, ss, rs, got):
            slots = slots_of(tree, rows)

            def edge(i):
                a, b, half, _ = slots[i]
                src = full.at[k, rows_of(base, n, -b, rows, half)]
                dst = full.at[k, rows_of(base, n, -a, rows, half)]
                return remote(src, dst, ss.at[k], rs.at[k, i], dev[(a - b) % n], x)

            def take(place):
                for i, (a, _, _, _) in enumerate(slots):
                    if a == place:
                        edge(i).wait_recv()
                        got(place)

            def send(lo, hi):
                done = set()
                for i in range(lo, hi):
                    b = slots[i][1]
                    if b not in done:
                        done.add(b)
                        if b != 0:
                            take(b)
                    edge(i).start()

            at = len(slots)
            for rnd in reversed(tree):
                steps.append(lambda lo=at - len(rnd), hi=at: send(lo, hi))
                at -= len(rnd)

            def rest():
                inner = {b for _, b, _, _ in slots}
                seen = set()
                for a, _, _, _ in slots:
                    if a not in inner and a not in seen:
                        seen.add(a)
                        take(a)

            return rest

        def chain(done, more):
            def both():
                done()
                more()

            return both

        end1 = sum_steps(BIG[first], n1, p1, dev1, 0, b1, rx1, sum_send, r1r)
        mark = len(steps)
        end2 = sum_steps(SMALL[second], n2, p2, dev2, base2, b2, rx2, sum_send, r2r)
        steps[mark] = chain(end1, steps[mark])
        mark = len(steps)

        def own():
            end2()
            at = rows_of(base2, n2, 0, b2, None)
            full[k, at, :] = mine[k, at, :]

        end3 = gather_steps(SMALL[second], n2, p2, dev2, base2, b2, gat_send, g2r, lambda place: None)
        steps[mark] = chain(own, steps[mark])
        mark = len(steps)

        sends = {}

        def forward(event, place, half):
            at = rows_of(0, n1, -place, b1, half)
            src = full.at[k, at, pl.ds(lcol, 128)]
            return [
                remote(src, left.at[at], fws.at[event, q - 1], fwr.at[event], c, lax.rem(x + q, NX))
                for q in range(1, NX)
            ]

        mine_to_send = jnp.logical_and(x == owner_x, lchunk == k)
        mine_to_get = jnp.logical_and(x != owner_x, lchunk == k)

        def out(place):
            sends[place] = len(sends)

            @pl.when(mine_to_send)
            def _():
                for cp in forward(sends[place], place, None):
                    cp.start()

        slots1 = slots_of(BIG[first], b1)
        counts = {}
        for a, _, _, _ in slots1:
            key = a % n1
            counts[key] = counts.get(key, 0) + 1
        left_over = dict(counts)

        def got(place):
            key = place % n1
            left_over[key] -= 1
            if left_over[key] == 0:
                out(key)

        def begin():
            end3()
            out(0)

        end4 = gather_steps(BIG[first], n1, p1, dev1, 0, b1, gat_send, g1r, got)
        steps[mark] = chain(begin, steps[mark])
        steps.append(end4)

        def finish():
            sent = pl.ds(0, HALF - b2)
            remote(mine.at[k, sent], mine.at[k, sent], sum_send.at[k], r1r.at[k, 0], c, x).wait_send()
            remote(full.at[k, sent], full.at[k, sent], gat_send.at[k], g1r.at[k, 0], c, x).wait_send()

            @pl.when(mine_to_send)
            def _():
                for place, event in sends.items():
                    for cp in forward(event, place, None):
                        cp.wait_send()
                left[...] = full[k, :, pl.ds(lcol, 128)]

            @pl.when(mine_to_get)
            def _():
                for place, event in sends.items():
                    at = rows_of(0, n1, -place, b1, None)
                    remote(left.at[at], left.at[at], fws.at[event, 0], fwr.at[event], c, x).wait_recv()

        return steps, finish, needs

    plans = [[plan(k, FIRST[h]) for k in range(CHUNKS)] for h in (0, 1)]

    def comm(k, s):
        for h in (0, 1):
            steps = plans[h][k][0]
            if s < len(steps):
                pl.when(core == h)(steps[s])

    units = HALF // UNIT
    made = folded = 0
    total = max(len(p[0]) for h in (0, 1) for p in plans[h])
    for s in range(total):
        upto = max(p[2][s] if s < len(p[2]) else HALF for h in (0, 1) for p in plans[h])
        upto = -(-upto // UNIT)
        ahead = min(units, max(upto + AHEAD, units if s else 0))
        while made < ahead:
            make(made)
            made += 1
        while folded < upto:
            fold(folded)
            folded += 1
        for k in range(CHUNKS):
            comm(k, s)
    for u in range(units):
        push(u).wait_send()
    for k in range(CHUNKS):
        for h in (0, 1):
            pl.when(core == h)(plans[h][k][1])

    lt = left[...].T
    lhi, llo = split(lt)
    lhs = jnp.concatenate([lhi, llo], axis=0)
    for n in range(CHUNKS):
        ghi, glo = split(full[n])
        both = jnp.dot(lhs, ghi, preferred_element_type=F32)
        low = jnp.dot(lhi, glo, preferred_element_type=F32)
        mpart[:, n * CW : (n + 1) * CW] = both[:128] + (both[128:] + low)
    ours = pl.ds(pl.multiple_of(core * 64, 64), 64)
    other = pl.ds(pl.multiple_of((1 - core) * 64, 64), 64)
    m = remote(mpart.at[other], mrx, m_send, m_recv, sib, x)
    m.start()
    m.wait()
    out_ref[...] = (mpart[ours, :] + mrx[...]) * F32(1.0 / 131072)


def per_device(features, coef, log_exposure, claims, cluster_id, period, period_effect):
    vmem = pl.BlockSpec(memory_space=pltpu.VMEM)
    dma = pltpu.SemaphoreType.DMA
    chunked = pltpu.VMEM((CHUNKS, HALF, CW), F32)
    scratch = [
        pltpu.VMEM((ROWS, WIDTH), BF16),
        pltpu.VMEM((16, WIDTH), BF16),
        pltpu.VMEM((NX, 16, 128), F32),
        pltpu.VMEM((16, 128), F32),
        pltpu.VMEM((2, HALF, ROWS), BF16),
        chunked,
        chunked,
        chunked,
        pltpu.VMEM((CHUNKS, 448, CW), F32),
        pltpu.VMEM((CHUNKS, 112, CW), F32),
        chunked,
        pltpu.VMEM((HALF, 128), F32),
        pltpu.VMEM((128, WIDTH), F32),
        pltpu.VMEM((64, WIDTH), F32),
        dma((FCH,)),
        dma((NX - 1,)),
        dma((NX - 1,)),
        dma((HALF // UNIT,)),
        dma((HALF // UNIT,)),
    ]
    scratch += [dma((CHUNKS,)) for _ in range(2)]
    scratch += [dma((CHUNKS, EDGES)) for _ in range(4)]
    scratch += [dma((8, NX - 1)), dma((8,)), dma, dma]
    return pl.pallas_call(
        kernel,
        out_shape=jax.ShapeDtypeStruct((64, WIDTH), F32),
        in_specs=[pl.BlockSpec(memory_space=pl.ANY)] + [vmem] * 6,
        out_specs=vmem,
        scratch_shapes=scratch,
        compiler_params=pltpu.CompilerParams(
            collective_id=0, has_side_effects=True, vmem_limit_bytes=56 << 20
        ),
    )(
        features,
        coef.reshape(8, 128),
        log_exposure.reshape(16, 128),
        claims.reshape(16, 128),
        cluster_id.reshape(16, 128),
        period.reshape(16, 128),
        period_effect.reshape(1, 128),
    )


def solution(mesh):
    placed = (P("cal", "gr"), P("gr"), P("cal"), P("cal"), P("cal"), P("cal"), P())
    return jax.shard_map(
        per_device, mesh=mesh, in_specs=placed, out_specs=P("cal", "gr"), check_vma=False
    )
```

```python
import jax
import jax.numpy as jnp
from jax import lax
from jax.experimental import pallas as pl
from jax.experimental.pallas import tpu as pltpu
from jax.sharding import PartitionSpec as P

NZ, NY, NX = 8, 4, 4
ROWS = 2048
WIDTH = 1024
HALF = 512
FCH = 4
CHUNKS = 4
CW = WIDTH // CHUNKS
RING4 = [[(2, 1, 0), (-2, -1, 1)], [(1, 0, None), (-1, 0, None)]]
DIRECT4 = [[(2, 0, None), (1, 0, None), (-1, 0, None)]]
RING8 = [[(4, 3, 0), (-4, -3, 1)]] + [[(k, k - 1, None), (-k, 1 - k, None)] for k in (3, 2, 1)]
THREE8 = [
    [(4, 2, 0), (-4, -2, 1), (3, 2, None), (-3, -2, None)],
    [(2, 1, None), (-2, -1, None)],
    [(1, 0, None), (-1, 0, None)],
]
TWO8 = [
    [(4, 2, 0), (-4, -2, 1), (3, 2, None), (-3, -2, None), (1, 0, None), (-1, 0, None)],
    [(2, 0, None), (-2, 0, None)],
]
DIRECT8 = [[(4, 0, None)] + [(s * k, 0, None) for k in (3, 2, 1) for s in (1, -1)]]
BIG_G = {"y": RING4, "z": RING8}
SMALL_G = {"y": DIRECT4, "z": TWO8}
BIG = {"y": RING4, "z": RING8}
SMALL = {"y": DIRECT4, "z": TWO8}
FIRST = "yz"
LAST = "zy"
UNIT = 128
EDGES = 8
F32 = jnp.float32
UNROLL = 4
AHEAD = 1
ZPEERS = (2, NZ - 2, 1, NZ - 1)
FARX = (2, 1, 3)
BF16 = jnp.bfloat16


def order(n):
    return [n // 2] + [w * d % n for d in range(n // 2 - 1, 0, -1) for w in (1, -1)] + [0]


def remote(src, dst, send, recv, cal, gr):
    return pltpu.make_async_remote_copy(
        src_ref=src,
        dst_ref=dst,
        send_sem=send,
        recv_sem=recv,
        device_id=(cal, gr),
        device_id_type=pl.DeviceIdType.MESH,
    )


def split(v):
    hi = v.astype(BF16)
    lo = (v - hi.astype(F32)).astype(BF16)
    return hi, lo


def kernel(
    feat_hbm, coef_ref, logexp_hbm, claims_hbm, ids_hbm, period_hbm, effect_hbm, out_ref,
    logexp_ref, claims_ref, ids_ref, period_ref, effect_ref, in_sem,
    feat, cbuf, lin, res, picks, theirs, mine, core_rx, rx1, rx2, full, left, mpart, mrx, high, low,
    feat_sem, lin_send, lin_recv, core_send, core_recv,
    sum_send, gat_send, r1r, r2r, g1r, g2r, fws, fwr, m_send, m_recv,
):
    c = lax.axis_index("cal")
    x = lax.axis_index("gr")
    core = lax.rem(c, 2)
    y = lax.rem(lax.div(c, 2), NY)
    z = lax.div(c, 2 * NY)
    sib = c + 1 - 2 * core

    def cal_of(zz, yy):
        return (zz * NY + yy) * 2 + core

    barrier = pltpu.get_barrier_semaphore()
    peers = [(cal_of(lax.rem(z + k, NZ), y), x) for k in ZPEERS]
    peers += [(cal_of(z, lax.rem(y + k, NY)), x) for k in (2, 1, NY - 1)]
    peers += [(c, lax.rem(x + k, NX)) for k in FARX]
    peers += [(sib, x)]
    for cal, gr in peers:
        pl.semaphore_signal(
            barrier, inc=1, device_id=(cal, gr), device_id_type=pl.DeviceIdType.MESH
        )

    small = [
        pltpu.make_async_copy(src, dst, in_sem.at[i])
        for i, (src, dst) in enumerate(
            [
                (logexp_hbm, logexp_ref),
                (claims_hbm, claims_ref),
                (ids_hbm, ids_ref),
                (period_hbm, period_ref),
                (effect_hbm, effect_ref),
            ]
        )
    ]
    fetches = []
    fr = ROWS // FCH
    for k in range(FCH):
        f = pltpu.make_async_copy(
            feat_hbm.at[pl.ds(k * fr, fr)], feat.at[pl.ds(k * fr, fr)], feat_sem.at[k]
        )
        f.start()
        fetches.append(f)
    for f in small:
        f.start()

    cf = coef_ref[...].astype(F32)
    for j in range(WIDTH // 128):
        cbuf[:, j * 128 : (j + 1) * 128] = jnp.broadcast_to(cf[j : j + 1, :], (16, 128)).astype(BF16)
    for k in range(FCH):
        fetches[k].wait()
        part = lax.dot_general(
            cbuf[...], feat[k * fr : (k + 1) * fr, :], (((1,), (1,)), ((), ())),
            preferred_element_type=F32,
        )
        for j in range(fr // 128):
            lin[x, k * (fr // 128) + j, :] = part[0, j * 128 : (j + 1) * 128]
    for f in small:
        f.wait()
    pl.semaphore_wait(barrier, len(peers))

    for k in FARX:
        to = lax.rem(x + k, NX)
        remote(lin.at[x], lin.at[x], lin_send.at[k - 1], lin_recv.at[k - 1], c, to).start()
    eff = effect_ref[...]
    where = lax.broadcasted_iota(jnp.int32, (1, 128), 1)
    d = c * 2
    e0 = jnp.sum(jnp.where(where == d, eff, 0.0), axis=1, keepdims=True)
    e1 = jnp.sum(jnp.where(where == d + 1, eff, 0.0), axis=1, keepdims=True)
    per = period_ref[...]
    shift = jnp.where(per == d, e0, jnp.where(per == d + 1, e1, 0.0))
    for k in range(1, NX):
        src = lax.rem(x + NX - k, NX)
        remote(lin.at[src], lin.at[src], lin_send.at[k - 1], lin_recv.at[k - 1], c, x).wait()
    linear = lin[0] + lin[1] + lin[2] + lin[3]
    value = claims_ref[...] - jnp.exp(linear + logexp_ref[...] + shift)
    res[...] = value.astype(BF16).astype(F32)

    ring_y = [lax.rem(y + k, NY) for k in range(NY)]
    ring_z = [lax.rem(z + k, NZ) for k in range(NZ)]
    axes = {
        "y": (NY, ring_y, [cal_of(z, q) for q in ring_y]),
        "z": (NZ, ring_z, [cal_of(q, y) for q in ring_z]),
    }

    def firsts(h):
        (n1, p1, _), (n2, p2, _) = axes[FIRST[h]], axes["z" if FIRST[h] == "y" else "y"]
        b1 = HALF // n1
        b2 = b1 // n2
        return [h * HALF + p1[d1] * b1 + p2[d2] * b2 for d1 in order(n1) for d2 in order(n2)]

    groups = [
        [jnp.where(core == half, v1, v0) for v0, v1 in zip(firsts(0), firsts(1))] for half in (0, 1)
    ]
    few = HALF // len(groups[0])

    def build(half, unit):
        def column(j, carry):
            row = lax.broadcasted_iota(jnp.int32, (few, 128), 0)
            ids = ids_ref[pl.ds(j, 1), :]
            val = jnp.broadcast_to(res[pl.ds(j, 1), :], (few, 128))
            col = pl.ds(pl.multiple_of(j * 128, 128), 128)
            for g in range(unit * UNIT // few, (unit + 1) * UNIT // few):
                hit = row == ids - groups[half][g]
                picks[half, g * few : (g + 1) * few, col] = jnp.where(hit, val, 0.0).astype(BF16)
            return carry

        lax.fori_loop(0, ROWS // 128, column, 0)

    def product(half, unit, dst):
        build(half, unit)
        here = slice(unit * UNIT, (unit + 1) * UNIT)
        wide = max(CW, 256)
        for n in range(0, WIDTH, wide):
            val = jnp.dot(picks[half, here, :], feat[:, n : n + wide], preferred_element_type=F32)
            for q in range(wide // CW):
                dst[n // CW + q, here, :] = val[:, q * CW : (q + 1) * CW]

    def push(u):
        here = pl.ds(u * UNIT, UNIT)
        return remote(
            theirs.at[:, here], core_rx.at[:, here], core_send.at[u], core_recv.at[u], sib, x
        )

    def make(u):
        product(0, u, theirs)
        push(u).start()
        product(1, u, mine)

    def fold(u):
        push(u).wait_recv()
        here = slice(u * UNIT, (u + 1) * UNIT)
        for n in range(CHUNKS):
            mine[n, here, :] += core_rx[n, here, :]

    owner_x = lax.div(z, 2)
    place = lax.rem(z, 2) * NY + y
    lchunk = lax.div(place, CW // 128)
    lcol = pl.multiple_of(lax.rem(place, CW // 128) * 128, 128)
    def rows_of(base, n, place, rows, half):
        start = base + order(n).index(place % n) * rows
        if half is not None:
            rows = rows // 2
            start = start + half * rows
        return pl.ds(start, rows)

    def slots_of(tree, rows):
        at, slots = 0, []
        for rnd in tree:
            for a, b, half in rnd:
                size = rows if half is None else rows // 2
                slots.append((a, b, half, pl.ds(at, size)))
                at += size
        return slots

    def add(k, start, rx, slot):
        def tile(j, carry):
            here = pl.ds(pl.multiple_of(start + j * 8, 8), 8)
            mine[k, here, :] += rx[k, pl.ds(pl.multiple_of(slot.start + j * 8, 8), 8), :]
            return carry

        lax.fori_loop(0, slot.size // 8, tile, 0, unroll=min(UNROLL, slot.size // 8))

    def plan(k, first, last):
        second = "z" if first == "y" else "y"
        n1, _, dev1 = axes[first]
        n2, _, dev2 = axes[second]
        b1 = HALF // n1
        b2 = b1 // n2
        base2 = HALF - b1
        needs = []
        steps = []

        def sum_steps(tree, n, dev, base, rows, rx, ss, rs):
            slots = slots_of(tree, rows)

            def edge(i):
                a, b, half, slot = slots[i]
                blk = rows_of(base, n, -a, rows, half)
                return remote(mine.at[k, blk], rx.at[k, slot], ss.at[k], rs.at[k, i], dev[(b - a) % n], x)

            def take(place):
                for i, (_, b, half, slot) in enumerate(slots):
                    if b == place:
                        edge(i).wait_recv()
                        add(k, rows_of(base, n, -b, rows, half).start, rx, slot)

            def send(lo, hi):
                done = set()
                for i in range(lo, hi):
                    a = slots[i][0]
                    if a not in done:
                        done.add(a)
                        take(a)
                    edge(i).start()

            at = 0
            for rnd in tree:
                blks = [rows_of(base, n, -a, rows, None) for a, _, _ in rnd]
                needs.append(max(blk.start + blk.size for blk in blks))
                steps.append(lambda lo=at, hi=at + len(rnd): send(lo, hi))
                at += len(rnd)
            return lambda: take(0)

        def gather_steps(tree, n, dev, base, rows, ss, rs, got):
            slots = slots_of(tree, rows)

            def edge(i):
                a, b, half, _ = slots[i]
                src = full.at[k, rows_of(base, n, -b, rows, half)]
                dst = full.at[k, rows_of(base, n, -a, rows, half)]
                return remote(src, dst, ss.at[k], rs.at[k, i], dev[(a - b) % n], x)

            def take(place):
                for i, (a, _, _, _) in enumerate(slots):
                    if a == place:
                        edge(i).wait_recv()
                        got(place)

            def send(lo, hi):
                done = set()
                for i in range(lo, hi):
                    b = slots[i][1]
                    if b not in done:
                        done.add(b)
                        if b != 0:
                            take(b)
                    edge(i).start()

            at = len(slots)
            for rnd in reversed(tree):
                steps.append(lambda lo=at - len(rnd), hi=at: send(lo, hi))
                at -= len(rnd)

            def rest():
                inner = {b for _, b, _, _ in slots}
                seen = set()
                for a, _, _, _ in slots:
                    if a not in inner and a not in seen:
                        seen.add(a)
                        take(a)

            return rest

        def chain(done, more):
            def both():
                done()
                more()

            return both

        end1 = sum_steps(BIG[first], n1, dev1, 0, b1, rx1, sum_send, r1r)
        mark = len(steps)
        end2 = sum_steps(SMALL[second], n2, dev2, base2, b2, rx2, sum_send, r2r)
        steps[mark] = chain(end1, steps[mark])
        mark = len(steps)

        inner = "z" if last == "y" else "y"
        m1, _, to1 = axes[last]
        m2, _, to2 = axes[inner]
        g1 = HALF // m1
        g2 = g1 // m2

        def own():
            end2()
            src = rows_of(base2, n2, 0, b2, None)
            full[k, rows_of(HALF - g1, m2, 0, g2, None), :] = mine[k, src, :]

        end3 = gather_steps(SMALL_G[inner], m2, to2, HALF - g1, g2, gat_send, g2r, lambda place: None)
        steps[mark] = chain(own, steps[mark])
        mark = len(steps)

        sends = {}

        def forward(event, place, half):
            at = rows_of(0, m1, -place, g1, half)
            src = full.at[k, at, pl.ds(lcol, 128)]
            return [
                remote(src, left.at[at], fws.at[event, q - 1], fwr.at[event], c, lax.rem(x + q, NX))
                for q in FARX
            ]

        mine_to_send = jnp.logical_and(x == owner_x, lchunk == k)
        mine_to_get = jnp.logical_and(x != owner_x, lchunk == k)

        def out(place):
            sends[place] = len(sends)

            @pl.when(mine_to_send)
            def _():
                for cp in forward(sends[place], place, None):
                    cp.start()

        slots1 = slots_of(BIG_G[last], g1)
        counts = {}
        for a, _, _, _ in slots1:
            key = a % m1
            counts[key] = counts.get(key, 0) + 1
        left_over = dict(counts)

        def got(place):
            key = place % m1
            left_over[key] -= 1
            if left_over[key] == 0:
                out(key)

        def begin():
            end3()
            out(0)

        end4 = gather_steps(BIG_G[last], m1, to1, 0, g1, gat_send, g1r, got)
        steps[mark] = chain(begin, steps[mark])
        steps.append(end4)

        def finish():
            sent = pl.ds(0, HALF - b2)
            remote(mine.at[k, sent], mine.at[k, sent], sum_send.at[k], r1r.at[k, 0], c, x).wait_send()
            remote(full.at[k, sent], full.at[k, sent], gat_send.at[k], g1r.at[k, 0], c, x).wait_send()

            @pl.when(mine_to_send)
            def _():
                for place, event in sends.items():
                    for cp in forward(event, place, None):
                        cp.wait_send()
                left[...] = full[k, :, pl.ds(lcol, 128)]

            @pl.when(mine_to_get)
            def _():
                for place, event in sends.items():
                    at = rows_of(0, m1, -place, g1, None)
                    remote(left.at[at], left.at[at], fws.at[event, 0], fwr.at[event], c, x).wait_recv()

        return steps, finish, needs

    plans = [[plan(k, FIRST[h], LAST[h]) for k in range(CHUNKS)] for h in (0, 1)]

    def comm(k, s):
        for h in (0, 1):
            steps = plans[h][k][0]
            if s < len(steps):
                pl.when(core == h)(steps[s])

    units = HALF // UNIT
    made = folded = 0
    total = max(len(p[0]) for h in (0, 1) for p in plans[h])
    for s in range(total):
        upto = max(p[2][s] if s < len(p[2]) else HALF for h in (0, 1) for p in plans[h])
        upto = -(-upto // UNIT)
        ahead = min(units, max(upto + AHEAD, units if s else 0))
        while made < ahead:
            make(made)
            made += 1
        while folded < upto:
            fold(folded)
            folded += 1
        for k in range(CHUNKS):
            comm(k, s)
            if s == total - 1:
                high[k], low[k] = split(full[k])
    for u in range(units):
        push(u).wait_send()
    for k in range(CHUNKS):
        for h in (0, 1):
            pl.when(core == h)(plans[h][k][1])

    lhi, llo = split(left[...].T)
    lhs = jnp.concatenate([lhi, llo], axis=0)
    for n in range(CHUNKS):
        both = jnp.dot(lhs, high[n], preferred_element_type=F32)
        rest = jnp.dot(lhi, low[n], preferred_element_type=F32)
        mpart[:, n * CW : (n + 1) * CW] = both[:128] + (both[128:] + rest)
    ours = pl.ds(pl.multiple_of(core * 64, 64), 64)
    other = pl.ds(pl.multiple_of((1 - core) * 64, 64), 64)
    m = remote(mpart.at[other], mrx, m_send, m_recv, sib, x)
    m.start()
    m.wait()
    out_ref[...] = (mpart[ours, :] + mrx[...]) * F32(1.0 / 131072)


def per_device(features, coef, log_exposure, claims, cluster_id, period, period_effect):
    vmem = pl.BlockSpec(memory_space=pltpu.VMEM)
    hbm = pl.BlockSpec(memory_space=pl.ANY)
    dma = pltpu.SemaphoreType.DMA
    chunked = pltpu.VMEM((CHUNKS, HALF, CW), F32)
    scratch = [
        pltpu.VMEM((16, 128), F32),
        pltpu.VMEM((16, 128), F32),
        pltpu.VMEM((16, 128), jnp.int32),
        pltpu.VMEM((16, 128), jnp.int32),
        pltpu.VMEM((1, 128), F32),
        dma((5,)),
        pltpu.VMEM((ROWS, WIDTH), BF16),
        pltpu.VMEM((16, WIDTH), BF16),
        pltpu.VMEM((NX, 16, 128), F32),
        pltpu.VMEM((16, 128), F32),
        pltpu.VMEM((2, HALF, ROWS), BF16),
        chunked,
        chunked,
        chunked,
        pltpu.VMEM((CHUNKS, 448, CW), F32),
        pltpu.VMEM((CHUNKS, 112, CW), F32),
        chunked,
        pltpu.VMEM((HALF, 128), F32),
        pltpu.VMEM((128, WIDTH), F32),
        pltpu.VMEM((64, WIDTH), F32),
        pltpu.VMEM((CHUNKS, HALF, CW), BF16),
        pltpu.VMEM((CHUNKS, HALF, CW), BF16),
        dma((FCH,)),
        dma((NX - 1,)),
        dma((NX - 1,)),
        dma((HALF // UNIT,)),
        dma((HALF // UNIT,)),
    ]
    scratch += [dma((CHUNKS,)) for _ in range(2)]
    scratch += [dma((CHUNKS, EDGES)) for _ in range(4)]
    scratch += [dma((8, NX - 1)), dma((8,)), dma, dma]
    return pl.pallas_call(
        kernel,
        out_shape=pltpu.VMEM((64, WIDTH), F32),
        in_specs=[hbm, vmem] + [hbm] * 5,
        out_specs=vmem,
        scratch_shapes=scratch,
        compiler_params=pltpu.CompilerParams(
            collective_id=0, has_side_effects=True, vmem_limit_bytes=56 << 20
        ),
    )(
        features,
        coef.reshape(8, 128),
        log_exposure.reshape(16, 128),
        claims.reshape(16, 128),
        cluster_id.reshape(16, 128),
        period.reshape(16, 128),
        period_effect.reshape(1, 128),
    )


def solution(mesh):
    placed = (P("cal", "gr"), P("gr"), P("cal"), P("cal"), P("cal"), P("cal"), P())
    return jax.shard_map(
        per_device, mesh=mesh, in_specs=placed, out_specs=P("cal", "gr"), check_vma=False
    )
```

```python
import jax
import jax.numpy as jnp
from jax import lax
from jax.experimental import pallas as pl
from jax.experimental.pallas import tpu as pltpu
from jax.sharding import PartitionSpec as P

NZ, NY, NX = 8, 4, 4
ROWS = 2048
WIDTH = 1024
HALF = 512
FCH = 4
CHUNKS = 4
CW = WIDTH // CHUNKS
RING4 = [[(2, 1, 0), (-2, -1, 1)], [(1, 0, None), (-1, 0, None)]]
DIRECT4 = [[(2, 0, None), (1, 0, None), (-1, 0, None)]]
RING8 = [[(4, 3, 0), (-4, -3, 1)]] + [[(k, k - 1, None), (-k, 1 - k, None)] for k in (3, 2, 1)]
THREE8 = [
    [(4, 2, 0), (-4, -2, 1), (3, 2, None), (-3, -2, None)],
    [(2, 1, None), (-2, -1, None)],
    [(1, 0, None), (-1, 0, None)],
]
TWO8 = [
    [(4, 2, 0), (-4, -2, 1), (3, 2, None), (-3, -2, None), (1, 0, None), (-1, 0, None)],
    [(2, 0, None), (-2, 0, None)],
]
DIRECT8 = [[(4, 0, None)] + [(s * k, 0, None) for k in (3, 2, 1) for s in (1, -1)]]
BIG_G = {"y": RING4, "z": RING8}
SMALL_G = {"y": DIRECT4, "z": TWO8}
BIG = {"y": RING4, "z": RING8}
SMALL = {"y": DIRECT4, "z": TWO8}
FIRST = "yz"
LAST = "yz"
UNIT = 128
EDGES = 8
F32 = jnp.float32
UNROLL = 4
AHEAD = 1
FARX = (2, 1, 3)
BF16 = jnp.bfloat16


def order(n):
    return [n // 2] + [w * d % n for d in range(n // 2 - 1, 0, -1) for w in (1, -1)] + [0]


def remote(src, dst, send, recv, cal, gr):
    return pltpu.make_async_remote_copy(
        src_ref=src,
        dst_ref=dst,
        send_sem=send,
        recv_sem=recv,
        device_id=(cal, gr),
        device_id_type=pl.DeviceIdType.MESH,
    )


def split(v):
    hi = v.astype(BF16)
    lo = (v - hi.astype(F32)).astype(BF16)
    return hi, lo


def kernel(
    feat_hbm, coef_ref, logexp_hbm, claims_hbm, ids_hbm, period_hbm, effect_hbm, out_ref,
    logexp_ref, claims_ref, ids_ref, period_ref, effect_ref, in_sem,
    feat, cbuf, lin, res, picks, theirs, mine, core_rx, rx1, rx2, full, left, mpart, mrx, high, low,
    feat_sem, lin_send, lin_recv, core_send, core_recv,
    sum_send, gat_send, r1r, r2r, g1r, g2r, fws, fwr, m_send, m_recv,
):
    c = lax.axis_index("cal")
    x = lax.axis_index("gr")
    core = lax.rem(c, 2)
    y = lax.rem(lax.div(c, 2), NY)
    z = lax.div(c, 2 * NY)
    sib = c + 1 - 2 * core

    def cal_of(zz, yy):
        return (zz * NY + yy) * 2 + core

    barrier = pltpu.get_barrier_semaphore()
    def greet(cal, gr):
        pl.semaphore_signal(
            barrier, inc=1, device_id=(cal, gr), device_id_type=pl.DeviceIdType.MESH
        )

    @pl.when(core == 0)
    def _():
        for k in (2, NZ - 2):
            greet(cal_of(lax.rem(z + k, NZ), y), x)

    @pl.when(core == 1)
    def _():
        greet(cal_of(z, lax.rem(y + 2, NY)), x)

    peers = [(cal_of(lax.rem(z + k, NZ), y), x) for k in (1, NZ - 1)]
    peers += [(cal_of(z, lax.rem(y + k, NY)), x) for k in (1, NY - 1)]
    peers += [(c, lax.rem(x + k, NX)) for k in FARX]
    peers += [(sib, x)]
    for cal, gr in peers:
        greet(cal, gr)

    small = [
        pltpu.make_async_copy(src, dst, in_sem.at[i])
        for i, (src, dst) in enumerate(
            [
                (logexp_hbm, logexp_ref),
                (claims_hbm, claims_ref),
                (ids_hbm, ids_ref),
                (period_hbm, period_ref),
                (effect_hbm, effect_ref),
            ]
        )
    ]
    fetches = []
    fr = ROWS // FCH
    for k in range(FCH):
        f = pltpu.make_async_copy(
            feat_hbm.at[pl.ds(k * fr, fr)], feat.at[pl.ds(k * fr, fr)], feat_sem.at[k]
        )
        f.start()
        fetches.append(f)
    for f in small:
        f.start()

    cf = coef_ref[...].astype(F32)
    for j in range(WIDTH // 128):
        cbuf[:, j * 128 : (j + 1) * 128] = jnp.broadcast_to(cf[j : j + 1, :], (16, 128)).astype(BF16)
    for k in range(FCH):
        fetches[k].wait()
        part = lax.dot_general(
            cbuf[...], feat[k * fr : (k + 1) * fr, :], (((1,), (1,)), ((), ())),
            preferred_element_type=F32,
        )
        for j in range(fr // 128):
            lin[x, k * (fr // 128) + j, :] = part[0, j * 128 : (j + 1) * 128]
    for f in small:
        f.wait()
    pl.semaphore_wait(barrier, len(peers) + 2 - core)

    for k in FARX:
        to = lax.rem(x + k, NX)
        remote(lin.at[x], lin.at[x], lin_send.at[k - 1], lin_recv.at[k - 1], c, to).start()
    eff = effect_ref[...]
    where = lax.broadcasted_iota(jnp.int32, (1, 128), 1)
    d = c * 2
    e0 = jnp.sum(jnp.where(where == d, eff, 0.0), axis=1, keepdims=True)
    e1 = jnp.sum(jnp.where(where == d + 1, eff, 0.0), axis=1, keepdims=True)
    per = period_ref[...]
    shift = jnp.where(per == d, e0, jnp.where(per == d + 1, e1, 0.0))
    for k in range(1, NX):
        src = lax.rem(x + NX - k, NX)
        remote(lin.at[src], lin.at[src], lin_send.at[k - 1], lin_recv.at[k - 1], c, x).wait()
    linear = lin[0] + lin[1] + lin[2] + lin[3]
    value = claims_ref[...] - jnp.exp(linear + logexp_ref[...] + shift)
    res[...] = value.astype(BF16).astype(F32)

    ring_y = [lax.rem(y + k, NY) for k in range(NY)]
    ring_z = [lax.rem(z + k, NZ) for k in range(NZ)]
    axes = {
        "y": (NY, ring_y, [cal_of(z, q) for q in ring_y]),
        "z": (NZ, ring_z, [cal_of(q, y) for q in ring_z]),
    }

    def firsts(h):
        (n1, p1, _), (n2, p2, _) = axes[FIRST[h]], axes["z" if FIRST[h] == "y" else "y"]
        b1 = HALF // n1
        b2 = b1 // n2
        return [h * HALF + p1[d1] * b1 + p2[d2] * b2 for d1 in order(n1) for d2 in order(n2)]

    groups = [
        [jnp.where(core == half, v1, v0) for v0, v1 in zip(firsts(0), firsts(1))] for half in (0, 1)
    ]
    few = HALF // len(groups[0])

    def build(half, unit):
        def column(j, carry):
            row = lax.broadcasted_iota(jnp.int32, (few, 128), 0)
            ids = ids_ref[pl.ds(j, 1), :]
            val = jnp.broadcast_to(res[pl.ds(j, 1), :], (few, 128))
            col = pl.ds(pl.multiple_of(j * 128, 128), 128)
            for g in range(unit * UNIT // few, (unit + 1) * UNIT // few):
                hit = row == ids - groups[half][g]
                picks[half, g * few : (g + 1) * few, col] = jnp.where(hit, val, 0.0).astype(BF16)
            return carry

        lax.fori_loop(0, ROWS // 128, column, 0)

    def product(half, unit, dst):
        build(half, unit)
        here = slice(unit * UNIT, (unit + 1) * UNIT)
        wide = max(CW, 256)
        for n in range(0, WIDTH, wide):
            val = jnp.dot(picks[half, here, :], feat[:, n : n + wide], preferred_element_type=F32)
            for q in range(wide // CW):
                dst[n // CW + q, here, :] = val[:, q * CW : (q + 1) * CW]

    def push(u):
        here = pl.ds(u * UNIT, UNIT)
        return remote(
            theirs.at[:, here], core_rx.at[:, here], core_send.at[u], core_recv.at[u], sib, x
        )

    def make(u):
        product(0, u, theirs)
        push(u).start()
        product(1, u, mine)

    def fold(u):
        push(u).wait_recv()
        here = slice(u * UNIT, (u + 1) * UNIT)
        for n in range(CHUNKS):
            mine[n, here, :] += core_rx[n, here, :]

    owner_x = lax.div(z, 2)
    place = lax.rem(z, 2) * NY + y
    lchunk = lax.div(place, CW // 128)
    lcol = pl.multiple_of(lax.rem(place, CW // 128) * 128, 128)
    def rows_of(base, n, place, rows, half):
        start = base + order(n).index(place % n) * rows
        if half is not None:
            rows = rows // 2
            start = start + half * rows
        return pl.ds(start, rows)

    def slots_of(tree, rows):
        at, slots = 0, []
        for rnd in tree:
            for a, b, half in rnd:
                size = rows if half is None else rows // 2
                slots.append((a, b, half, pl.ds(at, size)))
                at += size
        return slots

    def add(k, start, rx, slot):
        def tile(j, carry):
            here = pl.ds(pl.multiple_of(start + j * 8, 8), 8)
            mine[k, here, :] += rx[k, pl.ds(pl.multiple_of(slot.start + j * 8, 8), 8), :]
            return carry

        lax.fori_loop(0, slot.size // 8, tile, 0, unroll=min(UNROLL, slot.size // 8))

    def plan(k, first, last):
        second = "z" if first == "y" else "y"
        n1, _, dev1 = axes[first]
        n2, _, dev2 = axes[second]
        b1 = HALF // n1
        b2 = b1 // n2
        base2 = HALF - b1
        needs = []
        steps = []

        def sum_steps(tree, n, dev, base, rows, rx, ss, rs):
            slots = slots_of(tree, rows)

            def edge(i):
                a, b, half, slot = slots[i]
                blk = rows_of(base, n, -a, rows, half)
                return remote(mine.at[k, blk], rx.at[k, slot], ss.at[k], rs.at[k, i], dev[(b - a) % n], x)

            def take(place):
                for i, (_, b, half, slot) in enumerate(slots):
                    if b == place:
                        edge(i).wait_recv()
                        add(k, rows_of(base, n, -b, rows, half).start, rx, slot)

            def send(lo, hi):
                done = set()
                for i in range(lo, hi):
                    a = slots[i][0]
                    if a not in done:
                        done.add(a)
                        take(a)
                    edge(i).start()

            at = 0
            for rnd in tree:
                blks = [rows_of(base, n, -a, rows, None) for a, _, _ in rnd]
                needs.append(max(blk.start + blk.size for blk in blks))
                steps.append(lambda lo=at, hi=at + len(rnd): send(lo, hi))
                at += len(rnd)
            return lambda: take(0)

        def gather_steps(tree, n, dev, base, rows, ss, rs, got):
            slots = slots_of(tree, rows)

            def edge(i):
                a, b, half, _ = slots[i]
                src = full.at[k, rows_of(base, n, -b, rows, half)]
                dst = full.at[k, rows_of(base, n, -a, rows, half)]
                return remote(src, dst, ss.at[k], rs.at[k, i], dev[(a - b) % n], x)

            def take(place):
                for i, (a, _, _, _) in enumerate(slots):
                    if a == place:
                        edge(i).wait_recv()
                        got(place)

            def send(lo, hi):
                done = set()
                for i in range(lo, hi):
                    b = slots[i][1]
                    if b not in done:
                        done.add(b)
                        if b != 0:
                            take(b)
                    edge(i).start()

            at = len(slots)
            for rnd in reversed(tree):
                steps.append(lambda lo=at - len(rnd), hi=at: send(lo, hi))
                at -= len(rnd)

            def rest():
                inner = {b for _, b, _, _ in slots}
                seen = set()
                for a, _, _, _ in slots:
                    if a not in inner and a not in seen:
                        seen.add(a)
                        take(a)

            return rest

        def chain(done, more):
            def both():
                done()
                more()

            return both

        end1 = sum_steps(BIG[first], n1, dev1, 0, b1, rx1, sum_send, r1r)
        mark = len(steps)
        end2 = sum_steps(SMALL[second], n2, dev2, base2, b2, rx2, sum_send, r2r)
        steps[mark] = chain(end1, steps[mark])
        mark = len(steps)

        inner = "z" if last == "y" else "y"
        m1, _, to1 = axes[last]
        m2, _, to2 = axes[inner]
        g1 = HALF // m1
        g2 = g1 // m2

        def own():
            end2()
            src = rows_of(base2, n2, 0, b2, None)
            full[k, rows_of(HALF - g1, m2, 0, g2, None), :] = mine[k, src, :]

        end3 = gather_steps(SMALL_G[inner], m2, to2, HALF - g1, g2, gat_send, g2r, lambda place: None)
        steps[mark] = chain(own, steps[mark])
        mark = len(steps)

        sends = {}

        def forward(event, place, half):
            at = rows_of(0, m1, -place, g1, half)
            src = full.at[k, at, pl.ds(lcol, 128)]
            return [
                remote(src, left.at[at], fws.at[event, q - 1], fwr.at[event], c, lax.rem(x + q, NX))
                for q in FARX
            ]

        mine_to_send = jnp.logical_and(x == owner_x, lchunk == k)
        mine_to_get = jnp.logical_and(x != owner_x, lchunk == k)

        def out(place):
            sends[place] = len(sends)

            @pl.when(mine_to_send)
            def _():
                for cp in forward(sends[place], place, None):
                    cp.start()

        slots1 = slots_of(BIG_G[last], g1)
        counts = {}
        for a, _, _, _ in slots1:
            key = a % m1
            counts[key] = counts.get(key, 0) + 1
        left_over = dict(counts)

        def got(place):
            key = place % m1
            left_over[key] -= 1
            if left_over[key] == 0:
                out(key)

        def begin():
            end3()
            out(0)

        end4 = gather_steps(BIG_G[last], m1, to1, 0, g1, gat_send, g1r, got)
        steps[mark] = chain(begin, steps[mark])
        steps.append(end4)

        def finish():
            sent = pl.ds(0, HALF - b2)
            remote(mine.at[k, sent], mine.at[k, sent], sum_send.at[k], r1r.at[k, 0], c, x).wait_send()
            remote(full.at[k, sent], full.at[k, sent], gat_send.at[k], g1r.at[k, 0], c, x).wait_send()

            @pl.when(mine_to_send)
            def _():
                for place, event in sends.items():
                    for cp in forward(event, place, None):
                        cp.wait_send()
                left[...] = full[k, :, pl.ds(lcol, 128)]

            @pl.when(mine_to_get)
            def _():
                for place, event in sends.items():
                    at = rows_of(0, m1, -place, g1, None)
                    remote(left.at[at], left.at[at], fws.at[event, 0], fwr.at[event], c, x).wait_recv()

        return steps, finish, needs

    plans = [[plan(k, FIRST[h], LAST[h]) for k in range(CHUNKS)] for h in (0, 1)]

    def comm(k, s):
        for h in (0, 1):
            steps = plans[h][k][0]
            if s < len(steps):
                pl.when(core == h)(steps[s])

    units = HALF // UNIT
    made = folded = 0
    total = max(len(p[0]) for h in (0, 1) for p in plans[h])
    for s in range(total):
        upto = max(p[2][s] if s < len(p[2]) else HALF for h in (0, 1) for p in plans[h])
        upto = -(-upto // UNIT)
        ahead = min(units, max(upto + AHEAD, units if s else 0))
        while made < ahead:
            make(made)
            made += 1
        while folded < upto:
            fold(folded)
            folded += 1
        for k in range(CHUNKS):
            comm(k, s)
            if s == total - 1:
                high[k], low[k] = split(full[k])
    for u in range(units):
        push(u).wait_send()
    for k in range(CHUNKS):
        for h in (0, 1):
            pl.when(core == h)(plans[h][k][1])

    lhi, llo = split(left[...].T)
    lhs = jnp.concatenate([lhi, llo], axis=0)
    for n in range(CHUNKS):
        both = jnp.dot(lhs, high[n], preferred_element_type=F32)
        rest = jnp.dot(lhi, low[n], preferred_element_type=F32)
        mpart[:, n * CW : (n + 1) * CW] = both[:128] + (both[128:] + rest)
    ours = pl.ds(pl.multiple_of(core * 64, 64), 64)
    other = pl.ds(pl.multiple_of((1 - core) * 64, 64), 64)
    m = remote(mpart.at[other], mrx, m_send, m_recv, sib, x)
    m.start()
    m.wait()
    out_ref[...] = (mpart[ours, :] + mrx[...]) * F32(1.0 / 131072)


def per_device(features, coef, log_exposure, claims, cluster_id, period, period_effect):
    vmem = pl.BlockSpec(memory_space=pltpu.VMEM)
    hbm = pl.BlockSpec(memory_space=pl.ANY)
    dma = pltpu.SemaphoreType.DMA
    chunked = pltpu.VMEM((CHUNKS, HALF, CW), F32)
    scratch = [
        pltpu.VMEM((16, 128), F32),
        pltpu.VMEM((16, 128), F32),
        pltpu.VMEM((16, 128), jnp.int32),
        pltpu.VMEM((16, 128), jnp.int32),
        pltpu.VMEM((1, 128), F32),
        dma((5,)),
        pltpu.VMEM((ROWS, WIDTH), BF16),
        pltpu.VMEM((16, WIDTH), BF16),
        pltpu.VMEM((NX, 16, 128), F32),
        pltpu.VMEM((16, 128), F32),
        pltpu.VMEM((2, HALF, ROWS), BF16),
        chunked,
        chunked,
        chunked,
        pltpu.VMEM((CHUNKS, 448, CW), F32),
        pltpu.VMEM((CHUNKS, 112, CW), F32),
        chunked,
        pltpu.VMEM((HALF, 128), F32),
        pltpu.VMEM((128, WIDTH), F32),
        pltpu.VMEM((64, WIDTH), F32),
        pltpu.VMEM((CHUNKS, HALF, CW), BF16),
        pltpu.VMEM((CHUNKS, HALF, CW), BF16),
        dma((FCH,)),
        dma((NX - 1,)),
        dma((NX - 1,)),
        dma((HALF // UNIT,)),
        dma((HALF // UNIT,)),
    ]
    scratch += [dma((CHUNKS,)) for _ in range(2)]
    scratch += [dma((CHUNKS, EDGES)) for _ in range(4)]
    scratch += [dma((8, NX - 1)), dma((8,)), dma, dma]
    return pl.pallas_call(
        kernel,
        out_shape=pltpu.VMEM((64, WIDTH), F32),
        in_specs=[hbm, vmem] + [hbm] * 5,
        out_specs=vmem,
        scratch_shapes=scratch,
        compiler_params=pltpu.CompilerParams(
            collective_id=0, has_side_effects=True, vmem_limit_bytes=56 << 20
        ),
    )(
        features,
        coef.reshape(8, 128),
        log_exposure.reshape(16, 128),
        claims.reshape(16, 128),
        cluster_id.reshape(16, 128),
        period.reshape(16, 128),
        period_effect.reshape(1, 128),
    )


def solution(mesh):
    placed = (P("cal", "gr"), P("gr"), P("cal"), P("cal"), P("cal"), P("cal"), P())
    return jax.shard_map(
        per_device, mesh=mesh, in_specs=placed, out_specs=P("cal", "gr"), check_vma=False
    )
```
